32 devices in a mesh: tok: 8 (over z, y), feat: 4 (over x, core).
Axes of the slice: x: 2, y: 2, z: 4, core: 2. Of those that a mesh axis runs over, the one named last changes fastest.
Arguments:
- tokens: bfloat16 [128, 12288], P('tok', 'feat'), may hold values from -6 to 6
- up_weight: bfloat16 [4, 12288, 3, 3072], P('feat', 'tok'), may hold values from -0.0625 to 0.0625
- down_weight: bfloat16 [4, 12288, 3, 3072], P('feat', 'tok'), may hold values from -0.03125 to 0.03125
- up_left: bfloat16 [12288, 512], P('feat'), may hold values from -0.0546875 to 0.0546875
- up_right: bfloat16 [4, 12288, 512], P('feat', 'tok'), may hold values from -0.25 to 0.25
- down_left: bfloat16 [4, 12288, 512], P('feat', 'tok'), may hold values from -0.02734375 to 0.02734375
- down_right: bfloat16 [512, 12288], P(None, 'feat'), may hold values from -0.25 to 0.25
Outputs:
- mixed: bfloat16 [128, 12288], P('tok', 'feat')
The draws below stay inside these ranges and needn't reach their ends.
All inputs are finite; a program needn't handle non-finite values.
Results may differ from the reference program's by a relative error of at most 0.0058.
Values may be sent and summed in bfloat16 or wider, within the bound.
A program may use at most 128 MiB of HBM per device.

```python
import jax
import jax.numpy as jnp
import numpy as np
from jax import lax

D = 12288
FF = 49152
RANK = 512
TOKENS = 128
LEVELS = 2
DB = 3072
FFB = 12288
N_FEAT = 4


def steps_of(rng, dims, cuts, low, top_value):
    factor_of, own = 1.0, jax.random.fold_in(rng, 6)
    for dim, shards_of in cuts:
        heights = jnp.exp(jax.random.uniform(jax.random.fold_in(own, dim), (shards_of,), jnp.float32, low / len(cuts), top_value / len(cuts)))
        factor_of = factor_of * jnp.repeat(heights, dims[dim] // shards_of).reshape([-1 if axis == dim else 1 for axis in range(len(dims))])
    return factor_of


def centred(rng, shape, deviation, bound, split=(), kind=jnp.bfloat16):
    entries = deviation * jax.random.normal(rng, shape, jnp.float32)
    if split:
        entries = entries * steps_of(rng, shape, split, -0.22, 0.18)
    return jnp.clip(entries, -bound, bound).astype(kind)


def setup_inputs(seed: int = 0) -> dict:
    arg_keys = jax.random.split(jax.random.key(seed), 8)
    return {
        "tokens": centred(arg_keys[0], (TOKENS, D), 1.0, 6.0, ((0, 8), (1, 4))),
        "up_weight": centred(arg_keys[1], (N_FEAT, FFB, LEVELS + 1, DB), ((LEVELS + 1) * DB) ** -0.5, 0.0625, ((0, 4), (1, 8))),
        "down_weight": centred(arg_keys[2], (N_FEAT, FFB, LEVELS + 1, DB), ((LEVELS + 1) * FFB) ** -0.5, 0.03125, ((0, 4), (1, 8))),
        "up_left": centred(arg_keys[3], (D, RANK), D ** -0.5, 0.0546875, ((0, 4),)),
        "up_right": centred(arg_keys[4], (N_FEAT, FFB, RANK), RANK ** -0.5, 0.25, ((0, 4), (1, 8))),
        "down_left": centred(arg_keys[5], (N_FEAT, FFB, RANK), FF ** -0.5, 0.02734375, ((0, 4), (1, 8))),
        "down_right": centred(arg_keys[6], (RANK, D), RANK ** -0.5, 0.25, ((1, 4),)),
    }


def reference(tokens, up_weight, down_weight, up_left, up_right, down_left, down_right):
    table = jnp.array(np.array([[i ^ ((1 << k) >> 1) for k in range(LEVELS + 1)] for i in range(N_FEAT)]), dtype=jnp.int32)
    count = tokens.shape[0]
    blocks = tokens.reshape(count, N_FEAT, DB)
    code = jnp.dot(tokens, up_left, preferred_element_type=jnp.float32).astype(jnp.bfloat16)

    def up_block(index):
        inputs = jnp.take(blocks, table[index], axis=1).reshape(count, (LEVELS + 1) * DB)
        weights = up_weight[index].reshape(FFB, (LEVELS + 1) * DB)
        return jnp.dot(inputs, weights.T, preferred_element_type=jnp.float32)

    pre = lax.map(up_block, jnp.arange(N_FEAT, dtype=jnp.int32))
    pre = jnp.transpose(pre, (1, 0, 2)).reshape(count, FF)
    pre = pre + jnp.dot(code, up_right.reshape(FF, RANK).T, preferred_element_type=jnp.float32)
    hidden = jax.nn.gelu(pre, approximate=False).astype(jnp.bfloat16)
    hblocks = hidden.reshape(count, N_FEAT, FFB)

    def down_block(total, index):
        source = jnp.take(hblocks, index, axis=1)
        part = jnp.dot(source, down_weight[index].reshape(FFB, (LEVELS + 1) * DB), preferred_element_type=jnp.float32)
        return total.at[:, table[index]].add(part.reshape(count, LEVELS + 1, DB)), None

    start_total = jnp.zeros((count, N_FEAT, DB), jnp.float32)
    total, unused = lax.scan(down_block, start_total, jnp.arange(N_FEAT, dtype=jnp.int32))
    back = jnp.dot(hidden, down_left.reshape(FF, RANK), preferred_element_type=jnp.float32).astype(jnp.bfloat16)
    mixed = total.reshape(count, D) + jnp.dot(back, down_right, preferred_element_type=jnp.float32)
    return mixed.astype(jnp.bfloat16)
```

```python
import jax
import jax.numpy as jnp
from jax import lax
from jax.experimental import pallas as pl
from jax.experimental.pallas import tpu as pltpu
from jax.sharding import PartitionSpec as P

F32, BF16 = jnp.float32, jnp.bfloat16
MESH = pl.DeviceIdType.MESH
PLANES = 4
N_COPIES = 128


def nt_dot(a, b):
    return lax.dot_general(a, b, (((1,), (1,)), ((), ())), preferred_element_type=F32)


def gelu(x):
    return 0.5 * x * (1.0 + lax.erf(x * 0.7071067811865476))


def fused_kernel(
    tokens, up, down, up_left, up_right, down_left, down_right, out,
    blocks, weights, ul, ur, dl, dr, pre, hidden,
    code_in, code_own, code_all, back_out, back_in, feat_in, base,
    p2, p1, p1_in, q0, yout, xdiag, ydiag, xfull, yfull, zout, zin,
    send_sem, recv_sem, local_sem,
):
    rows = tokens.shape[0]
    db, units = up.shape[2], up.shape[1]
    half = db // 2
    tok, feat = lax.axis_index("tok"), lax.axis_index("feat")
    z, y = lax.div(tok, 2), lax.rem(tok, 2)
    oy = 1 - y

    def fetch(n, src, dst):
        copy = pltpu.make_async_copy(src, dst, local_sem.at[n])
        copy.start()
        return copy

    got_tokens = fetch(0, tokens, blocks.at[0, tok])
    got_ul = fetch(1, up_left, ul)
    got_up = [fetch(2 + k, up.at[k], weights.at[k]) for k in range(3)]
    got_ur = fetch(5, up_right, ur)
    got_dl = fetch(6, down_left, dl)
    got_down = {2: fetch(7, down.at[2], weights.at[3])}
    got_dr = fetch(8, down_right, dr)

    def tok_peer(e):
        return {"tok": lax.bitwise_xor(tok, e), "feat": feat}

    def feat_peer(e):
        return {"tok": tok, "feat": lax.bitwise_xor(feat, e)}

    to_y, to_x, to_sib = tok_peer(1), feat_peer(2), feat_peer(1)
    barrier = pltpu.get_barrier_semaphore()
    peers = [tok_peer(e) for e in range(1, 2 * PLANES)] + [feat_peer(e) for e in range(1, 4)]
    for peer in peers:
        pl.semaphore_signal(barrier, inc=1, device_id=peer, device_id_type=MESH)
    pl.semaphore_wait(barrier, len(peers))

    sent = []

    def send(src, dst, peer):
        n = len(sent)
        copy = pltpu.make_async_remote_copy(
            src_ref=src, dst_ref=dst, send_sem=send_sem.at[n], recv_sem=recv_sem.at[n],
            device_id=peer, device_id_type=MESH)
        copy.start()
        sent.append(copy)
        return copy

    h0, h1 = pl.ds(0, half), pl.ds(half, half)
    ys, xs, zs, sibs, diag = {}, {}, {}, [], []

    def spread(src, t, d):
        ys[d] = send(src, blocks.at[0, t], to_y)
        xs[d] = send(src, blocks.at[2, t], to_x)
        sibs.append(send(src, blocks.at[1, t], to_sib))

    def at(d, row):
        return 2 * lax.bitwise_xor(z, d) + row

    spread(tokens, tok, 0)
    for d in range(1, PLANES):
        zs[d] = send(tokens, blocks.at[0, tok], tok_peer(2 * d))
    got_tokens.wait()
    got_ul.wait()
    code_in[feat] = jnp.dot(blocks[0, tok], ul[...], preferred_element_type=F32)
    code_parts = [send(code_in.at[feat], code_in.at[feat], feat_peer(e)) for e in range(1, 4)]

    def from_z(d):
        zs[d].wait_recv()
        t = at(d, y)
        spread(blocks.at[0, t], t, d)

    def from_yx(d):
        ys[d].wait_recv()
        t = at(d, oy)
        sibs.append(send(blocks.at[0, t], blocks.at[1, t], to_sib))
        diag.append(send(blocks.at[0, t, :, h0], blocks.at[2, t, :, h0], to_x))
        xs[d].wait_recv()
        t = at(d, y)
        diag.append(send(blocks.at[2, t, :, h1], blocks.at[2, t, :, h1], to_y))

    from_z(1)
    from_yx(0)
    from_z(2)
    for copy in code_parts:
        copy.wait_recv()
    code_all[tok] = (code_in[0] + code_in[1] + code_in[2] + code_in[3]).astype(BF16)
    codes = [send(code_all.at[tok], code_all.at[tok], tok_peer(e)) for e in range(1, 2 * PLANES)]
    from_yx(1)
    from_z(3)
    from_yx(2)
    from_yx(3)

    step = 256
    count = 2 * PLANES * rows

    def up_part(k, finish):
        got_up[k].wait()

        def body(j, carry):
            part = pl.ds(pl.multiple_of(j * step, step), step)
            value = nt_dot(blocks[k].reshape(count, db), weights[k, part, :])
            finish(part, value)
            return carry

        lax.fori_loop(0, units // step, body, 0)

    def first(part, value):
        pre[:, part] = value

    def more(part, value):
        pre[:, part] += value

    def last(part, value):
        low_rank = nt_dot(code_all[...].reshape(count, -1), ur[part, :])
        hidden[:, part] = gelu(pre[:, part] + value + low_rank).astype(BF16)

    up_part(0, first)
    got_down[1] = fetch(9, down.at[1], weights.at[0])
    for copy in sibs:
        copy.wait_recv()
    up_part(1, more)
    got_down[0] = fetch(10, down.at[0], weights.at[1])
    for copy in diag + codes:
        copy.wait_recv()
    got_ur.wait()
    up_part(2, last)

    got_dl.wait()
    back_out[...] = jnp.dot(
        hidden[...], dl[...], preferred_element_type=F32).astype(BF16).reshape(back_out.shape)
    backs = []
    for e in range(1, 2 * PLANES):
        other = lax.bitwise_xor(tok, e)
        backs.append(send(back_out.at[other], back_in.at[e], tok_peer(e)))

    width = 512
    n_half = half // width
    order = [c + s * n_half for c in range(n_half) for s in range(2)]
    slots = {2: 3, 1: 0, 0: 1}

    def cols_of(c):
        return pl.ds(c * width, width)

    def down_part(k, c):
        value = jnp.dot(hidden[...], weights[slots[k], :, cols_of(c)], preferred_element_type=F32)
        return value.reshape(PLANES, 2, rows, width)

    xd, yd, xf, yf, sib = {}, {}, {}, {}, {}
    got_down[2].wait()
    for c in order:
        cols = cols_of(c)
        p2[:, :, :, cols] = down_part(2, c).astype(BF16)
        if c < n_half:
            xd[c] = send(p2.at[:, oy, :, cols], xdiag.at[:, :, cols], to_x)
            xf[c] = send(p2.at[:, y, :, cols], xfull.at[:, :, cols], to_x)
        else:
            there = pl.ds(c * width - half, width)
            yd[c] = send(p2.at[:, oy, :, cols], ydiag.at[:, :, there], to_y)
    got_down[1].wait()
    for c in order:
        cols = cols_of(c)
        p1[:, :, :, cols] = down_part(1, c).astype(BF16)
        sib[c] = send(p1.at[:, :, :, cols], p1_in.at[:, :, :, cols], to_sib)
        if c >= n_half:
            here = pl.ds(c * width - half, width)
            yd[c].wait_recv()
            total = p2[:, y, :, cols].astype(F32) + ydiag[:, :, here].astype(F32)
            p2[:, y, :, cols] = total.astype(BF16)
            xf[c] = send(p2.at[:, y, :, cols], xfull.at[:, :, cols], to_x)
    got_down[0].wait()
    for c in order:
        cols = cols_of(c)
        value = down_part(0, c)
        sib[c].wait_recv()
        q0[:, :, :, cols] = value + p1_in[:, :, :, cols].astype(F32)
        away = q0[:, oy, :, cols]
        if c < n_half:
            xd[c].wait_recv()
            away = away + xdiag[:, :, cols].astype(F32)
        yout[:, :, cols] = away.astype(BF16)
        yf[c] = send(yout.at[:, :, cols], yfull.at[:, :, cols], to_y)

    for copy in backs:
        copy.wait_recv()
    total = back_out[tok].astype(F32)
    for e in range(1, 2 * PLANES):
        total = total + back_in[e].astype(F32)
    feat_in[feat] = total
    back_parts = [send(feat_in.at[feat], feat_in.at[feat], feat_peer(e)) for e in range(1, 4)]

    zf = {}
    for c in order:
        cols = cols_of(c)
        xf[c].wait_recv()
        yf[c].wait_recv()
        total = q0[:, y, :, cols] + xfull[:, :, cols].astype(F32) + yfull[:, :, cols].astype(F32)
        q0[:, y, :, cols] = total
        zout[:, :, cols] = total.astype(BF16)
        for d in range(1, PLANES):
            zf[c, d] = send(
                zout.at[lax.bitwise_xor(z, d), :, cols], zin.at[d, :, cols], tok_peer(2 * d))

    for copy in back_parts:
        copy.wait_recv()
    back = (feat_in[0] + feat_in[1] + feat_in[2] + feat_in[3]).astype(BF16)
    got_dr.wait()
    base[...] = jnp.dot(back, dr[...], preferred_element_type=F32)
    for c in order:
        cols = cols_of(c)
        total = q0[z, y, :, cols] + base[:, cols]
        for d in range(1, PLANES):
            zf[c, d].wait_recv()
            total = total + zin[d, :, cols].astype(F32)
        out[:, cols] = total.astype(BF16)
    for copy in sent:
        copy.wait_send()


def fused(tokens, up_weight, down_weight, up_left, up_right, down_left, down_right):
    rows, db = tokens.shape
    units = up_weight.shape[1]
    rank = up_left.shape[1]
    n = 2 * PLANES
    anywhere = pl.BlockSpec(memory_space=pl.ANY)
    vm = pltpu.VMEM
    return pl.pallas_call(
        fused_kernel,
        out_shape=jax.ShapeDtypeStruct((rows, db), BF16),
        in_specs=[anywhere] * 7,
        out_specs=pl.BlockSpec(memory_space=pltpu.VMEM),
        scratch_shapes=[
            vm((3, n, rows, db), BF16),
            vm((4, units, db), BF16),
            vm((db, rank), BF16),
            vm((units, rank), BF16),
            vm((units, rank), BF16),
            vm((rank, db), BF16),
            vm((n * rows, units), F32),
            vm((n * rows, units), BF16),
            vm((4, rows, rank), F32),
            vm((rows, rank), F32),
            vm((n, rows, rank), BF16),
            vm((n, rows, rank), BF16),
            vm((n, rows, rank), BF16),
            vm((4, rows, rank), F32),
            vm((rows, db), F32),
            vm((PLANES, 2, rows, db), BF16),
            vm((PLANES, 2, rows, db), BF16),
            vm((PLANES, 2, rows, db), BF16),
            vm((PLANES, 2, rows, db), F32),
            vm((PLANES, rows, db), BF16),
            vm((PLANES, rows, db // 2), BF16),
            vm((PLANES, rows, db // 2), BF16),
            vm((PLANES, rows, db), BF16),
            vm((PLANES, rows, db), BF16),
            vm((PLANES, rows, db), BF16),
            vm((PLANES, rows, db), BF16),
            pltpu.SemaphoreType.DMA((N_COPIES,)),
            pltpu.SemaphoreType.DMA((N_COPIES,)),
            pltpu.SemaphoreType.DMA((11,)),
        ],
        compiler_params=pltpu.CompilerParams(
            collective_id=0, has_side_effects=True, vmem_limit_bytes=63 * 2**20),
        name="butterfly",
    )(
        tokens,
        jnp.transpose(up_weight[0], (1, 0, 2)),
        jnp.transpose(down_weight[0], (1, 0, 2)),
        up_left, up_right[0], down_left[0], down_right,
    )


def from_partner(array, axis, bit):
    return lax.ppermute(array, axis, [(i, i ^ 1 << bit) for i in range(lax.axis_size(axis))])


def general(tokens, up_weight, down_weight, up_left, up_right, down_left, down_right):
    levels = lax.axis_size("feat").bit_length() - 1
    gathered = lax.all_gather(tokens, "tok", axis=0, tiled=True)
    pieces = [gathered]
    for level in range(levels):
        pieces.append(from_partner(gathered, "feat", level))
    stacked = jnp.stack(pieces, axis=1)
    code_part = jnp.dot(tokens, up_left, preferred_element_type=jnp.float32)
    code = lax.psum(code_part, "feat").astype(jnp.bfloat16)
    code = lax.all_gather(code, "tok", axis=0, tiled=True)
    pre = jnp.einsum("rkd,tkd->rt", up_weight[0], stacked, preferred_element_type=jnp.float32)
    pre = pre + lax.dot_general(
        up_right[0], code, (((1,), (1,)), ((), ())), preferred_element_type=jnp.float32
    )
    hidden = jax.nn.gelu(pre, approximate=False).astype(jnp.bfloat16)
    local_down = down_weight[0]
    terms = jnp.einsum("rt,rkd->tkd", hidden, local_down, preferred_element_type=jnp.float32)
    total = terms[:, 0, :]
    for level in range(levels):
        total = total + from_partner(terms[:, level + 1, :], "feat", level)
    back_part = lax.dot_general(
        hidden, down_left[0], (((0,), (0,)), ((), ())), preferred_element_type=jnp.float32
    )
    total, back = (
        lax.psum_scatter(total, "tok", scatter_dimension=0, tiled=True),
        lax.psum_scatter(back_part, "tok", scatter_dimension=0, tiled=True),
    )
    back = lax.psum(back, "feat")
    mixed = total + jnp.dot(
        back.astype(jnp.bfloat16), down_right, preferred_element_type=jnp.float32
    )
    return mixed.astype(jnp.bfloat16)


def per_device(tokens, up_weight, *rest):
    rows, db = tokens.shape
    small = (lax.axis_size("tok"), lax.axis_size("feat")) == (2 * PLANES, 4)
    fits = rows % 16 == 0 and db % 1024 == 0 and up_weight.shape[1] % 256 == 0
    fits = fits and up_weight.shape[1] * db * 8 <= 40 * 2**20
    form = fused if small and fits else general
    return form(tokens, up_weight, *rest)


def solution(mesh):
    return jax.shard_map(
        per_device,
        mesh=mesh,
        in_specs=(
            P("tok", "feat"),
            P("feat", "tok", None, None),
            P("feat", "tok", None, None),
            P("feat", None),
            P("feat", "tok", None),
            P("feat", "tok", None),
            P(None, "feat"),
        ),
        out_specs=P("tok", "feat"),
        check_vma=False,
    )
```

```python
import jax
import jax.numpy as jnp
from jax import lax
from jax.experimental import pallas as pl
from jax.experimental.pallas import tpu as pltpu
from jax.sharding import PartitionSpec as P

F32, BF16 = jnp.float32, jnp.bfloat16
MESH = pl.DeviceIdType.MESH
PLANES = 4
N_COPIES = 128


def nt_dot(a, b):
    return lax.dot_general(a, b, (((1,), (1,)), ((), ())), preferred_element_type=F32)


def gelu(x):
    return 0.5 * x * (1.0 + lax.erf(x * 0.7071067811865476))


def fused_kernel(
    tokens, up, down, up_left, up_right, down_left, down_right, out,
    blocks, weights, ul, ur, dl, dr, pre, hidden,
    code_in, code_all, back_out, back_in, feat_in, base,
    p2, p1, p1_in, q0, yout, xdiag, ydiag, xfull, yfull, zout, zin,
    send_sem, recv_sem, line_send, line_recv, local_sem,
):
    rows = tokens.shape[0]
    db, units = up.shape[2], up.shape[1]
    half = db // 2
    tok, feat = lax.axis_index("tok"), lax.axis_index("feat")
    z, y = lax.div(tok, 2), lax.rem(tok, 2)
    oy = 1 - y

    def fetch(n, src, dst):
        copy = pltpu.make_async_copy(src, dst, local_sem.at[n])
        copy.start()
        return copy

    got_tokens = fetch(0, tokens, blocks.at[0, tok])
    got_ul = fetch(1, up_left, ul)
    got_up = [fetch(2 + k, up.at[k], weights.at[k]) for k in range(3)]
    got_ur = fetch(5, up_right, ur)
    got_dl = fetch(6, down_left, dl)
    got_down = {2: fetch(7, down.at[2], weights.at[3])}
    got_dr = fetch(8, down_right, dr)

    def tok_peer(e):
        return {"tok": lax.bitwise_xor(tok, e), "feat": feat}

    def feat_peer(e):
        return {"tok": tok, "feat": lax.bitwise_xor(feat, e)}

    to_y, to_x, to_sib = tok_peer(1), feat_peer(2), feat_peer(1)
    barrier = pltpu.get_barrier_semaphore()
    peers = [tok_peer(e) for e in range(1, 2 * PLANES)] + [feat_peer(e) for e in range(1, 4)]
    for peer in peers:
        pl.semaphore_signal(barrier, inc=1, device_id=peer, device_id_type=MESH)
    pl.semaphore_wait(barrier, len(peers))

    sent = []

    def send(src, dst, peer):
        n = len(sent)
        copy = pltpu.make_async_remote_copy(
            src_ref=src, dst_ref=dst, send_sem=send_sem.at[n], recv_sem=recv_sem.at[n],
            device_id=peer, device_id_type=MESH)
        copy.start()
        sent.append(copy)
        return copy

    h0, h1 = pl.ds(0, half), pl.ds(half, half)
    ys, xs, sibs, diag = [], [], [], []
    middle = jnp.logical_or(z == 1, z == 2)

    planes = [
        z,
        lax.bitwise_xor(z, 1),
        lax.bitwise_xor(z, jnp.where(middle, 3, 2)),
        lax.bitwise_xor(z, jnp.where(middle, 2, 3)),
    ]
    near, across = tok_peer(2), tok_peer(6)

    def along(n, j, src, dst, peer):
        return pltpu.make_async_remote_copy(
            src_ref=src, dst_ref=dst, send_sem=line_send.at[n], recv_sem=line_recv.at[j],
            device_id=peer, device_id_type=MESH)

    def spread(src, t):
        ys.append(send(src, blocks.at[0, t], to_y))
        xs.append(send(src, blocks.at[2, t], to_x))
        sibs.append(send(src, blocks.at[1, t], to_sib))

    own = blocks.at[0, tok]
    shards = [blocks.at[0, 2 * plane + y] for plane in planes]
    pair = along(0, 0, tokens, own, near)
    pair.start()
    relays = [
        along(1, 1, tokens, own, across),
        along(2, 2, shards[1], shards[1], across),
        along(3, 1, shards[2], shards[2], near),
        along(4, 2, shards[3], shards[3], near),
    ]

    def relay(n):
        pl.when(middle)(lambda: relays[n].start())

    relay(0)
    spread(tokens, tok)
    got_tokens.wait()
    got_ul.wait()
    code_in[feat] = jnp.dot(blocks[0, tok], ul[...], preferred_element_type=F32)
    code_parts = [send(code_in.at[feat], code_in.at[feat], feat_peer(e)) for e in range(1, 4)]
    pair.wait_recv()
    relay(1)
    spread(shards[1], 2 * planes[1] + y)
    relays[0].wait_recv()
    relay(2)
    spread(shards[2], 2 * planes[2] + y)
    relays[1].wait_recv()
    relay(3)
    spread(shards[3], 2 * planes[3] + y)
    for j in range(PLANES):
        ys[j].wait_recv()
        t = 2 * planes[j] + oy
        sibs.append(send(blocks.at[0, t], blocks.at[1, t], to_sib))
        diag.append(send(blocks.at[0, t, :, h0], blocks.at[2, t, :, h0], to_x))
        xs[j].wait_recv()
        t = 2 * planes[j] + y
        diag.append(send(blocks.at[2, t, :, h1], blocks.at[2, t, :, h1], to_y))

    for copy in code_parts:
        copy.wait_recv()
    code_all[tok] = (code_in[0] + code_in[1] + code_in[2] + code_in[3]).astype(BF16)
    codes = [send(code_all.at[tok], code_all.at[tok], tok_peer(e)) for e in range(1, 2 * PLANES)]

    step = 256
    count = 2 * PLANES * rows

    def up_part(k, finish):
        got_up[k].wait()

        def body(j, carry):
            part = pl.ds(pl.multiple_of(j * step, step), step)
            value = nt_dot(blocks[k].reshape(count, db), weights[k, part, :])
            finish(part, value)
            return carry

        lax.fori_loop(0, units // step, body, 0)

    def first(part, value):
        pre[:, part] = value

    def more(part, value):
        pre[:, part] += value

    def last(part, value):
        low_rank = nt_dot(code_all[...].reshape(count, -1), ur[part, :])
        hidden[:, part] = gelu(pre[:, part] + value + low_rank).astype(BF16)

    up_part(0, first)
    got_down[1] = fetch(9, down.at[1], weights.at[0])
    for copy in sibs:
        copy.wait_recv()
    up_part(1, more)
    got_down[0] = fetch(10, down.at[0], weights.at[1])
    for copy in diag + codes:
        copy.wait_recv()
    got_ur.wait()
    up_part(2, last)

    width = 512
    n_half = half // width
    order = [c + s * n_half for c in range(n_half) for s in range(2)]
    slots = {2: 3, 1: 0, 0: 1}

    def cols_of(c):
        return pl.ds(c * width, width)

    def down_part(k, c):
        value = jnp.dot(hidden[...], weights[slots[k], :, cols_of(c)], preferred_element_type=F32)
        return value.reshape(PLANES, 2, rows, width)

    xd, yd, xf, yf, sib = {}, {}, {}, {}, {}
    got_down[2].wait()
    for c in order:
        cols = cols_of(c)
        p2[:, :, :, cols] = down_part(2, c).astype(BF16)
        if c < n_half:
            xd[c] = send(p2.at[:, oy, :, cols], xdiag.at[:, :, cols], to_x)
            xf[c] = send(p2.at[:, y, :, cols], xfull.at[:, :, cols], to_x)
        else:
            there = pl.ds(c * width - half, width)
            yd[c] = send(p2.at[:, oy, :, cols], ydiag.at[:, :, there], to_y)
    got_dl.wait()
    back_out[...] = jnp.dot(
        hidden[...], dl[...], preferred_element_type=F32).astype(BF16).reshape(back_out.shape)
    backs = []
    for e in range(1, 2 * PLANES):
        other = lax.bitwise_xor(tok, e)
        backs.append(send(back_out.at[other], back_in.at[e], tok_peer(e)))

    got_down[1].wait()
    for c in order:
        cols = cols_of(c)
        p1[:, :, :, cols] = down_part(1, c).astype(BF16)
        sib[c] = send(p1.at[:, :, :, cols], p1_in.at[:, :, :, cols], to_sib)
        if c >= n_half:
            here = pl.ds(c * width - half, width)
            yd[c].wait_recv()
            total = p2[:, y, :, cols].astype(F32) + ydiag[:, :, here].astype(F32)
            p2[:, y, :, cols] = total.astype(BF16)
            xf[c] = send(p2.at[:, y, :, cols], xfull.at[:, :, cols], to_x)
    got_down[0].wait()
    for c in order:
        cols = cols_of(c)
        value = down_part(0, c)
        sib[c].wait_recv()
        q0[:, :, :, cols] = value + p1_in[:, :, :, cols].astype(F32)
        away = q0[:, oy, :, cols]
        if c < n_half:
            xd[c].wait_recv()
            away = away + xdiag[:, :, cols].astype(F32)
        yout[:, :, cols] = away.astype(BF16)
        yf[c] = send(yout.at[:, :, cols], yfull.at[:, :, cols], to_y)

    for copy in backs:
        copy.wait_recv()
    total = back_out[tok].astype(F32)
    for e in range(1, 2 * PLANES):
        total = total + back_in[e].astype(F32)
    feat_in[feat] = total
    back_parts = [send(feat_in.at[feat], feat_in.at[feat], feat_peer(e)) for e in range(1, 4)]

    zf = {}
    for c in order:
        cols = cols_of(c)
        xf[c].wait_recv()
        yf[c].wait_recv()
        total = q0[:, y, :, cols] + xfull[:, :, cols].astype(F32) + yfull[:, :, cols].astype(F32)
        q0[:, y, :, cols] = total
        zout[:, :, cols] = total.astype(BF16)
        for d in range(1, PLANES):
            zf[c, d] = send(
                zout.at[lax.bitwise_xor(z, d), :, cols], zin.at[d, :, cols], tok_peer(2 * d))

    for copy in back_parts:
        copy.wait_recv()
    back = (feat_in[0] + feat_in[1] + feat_in[2] + feat_in[3]).astype(BF16)
    got_dr.wait()
    base[...] = jnp.dot(back, dr[...], preferred_element_type=F32)
    for c in order:
        cols = cols_of(c)
        total = q0[z, y, :, cols] + base[:, cols]
        for d in range(1, PLANES):
            zf[c, d].wait_recv()
            total = total + zin[d, :, cols].astype(F32)
        out[:, cols] = total.astype(BF16)
    pair.wait_send()

    @pl.when(middle)
    def _():
        for copy in relays:
            copy.wait_send()

    for copy in sent:
        copy.wait_send()


def fused(tokens, up_weight, down_weight, up_left, up_right, down_left, down_right):
    rows, db = tokens.shape
    units = up_weight.shape[1]
    rank = up_left.shape[1]
    n = 2 * PLANES
    anywhere = pl.BlockSpec(memory_space=pl.ANY)
    vm = pltpu.VMEM
    return pl.pallas_call(
        fused_kernel,
        out_shape=jax.ShapeDtypeStruct((rows, db), BF16),
        in_specs=[anywhere] * 7,
        out_specs=pl.BlockSpec(memory_space=pltpu.VMEM),
        scratch_shapes=[
            vm((3, n, rows, db), BF16),
            vm((4, units, db), BF16),
            vm((db, rank), BF16),
            vm((units, rank), BF16),
            vm((units, rank), BF16),
            vm((rank, db), BF16),
            vm((n * rows, units), F32),
            vm((n * rows, units), BF16),
            vm((4, rows, rank), F32),
            vm((n, rows, rank), BF16),
            vm((n, rows, rank), BF16),
            vm((n, rows, rank), BF16),
            vm((4, rows, rank), F32),
            vm((rows, db), F32),
            vm((PLANES, 2, rows, db), BF16),
            vm((PLANES, 2, rows, db), BF16),
            vm((PLANES, 2, rows, db), BF16),
            vm((PLANES, 2, rows, db), F32),
            vm((PLANES, rows, db), BF16),
            vm((PLANES, rows, db // 2), BF16),
            vm((PLANES, rows, db // 2), BF16),
            vm((PLANES, rows, db), BF16),
            vm((PLANES, rows, db), BF16),
            vm((PLANES, rows, db), BF16),
            vm((PLANES, rows, db), BF16),
            pltpu.SemaphoreType.DMA((N_COPIES,)),
            pltpu.SemaphoreType.DMA((N_COPIES,)),
            pltpu.SemaphoreType.DMA((5,)),
            pltpu.SemaphoreType.DMA((3,)),
            pltpu.SemaphoreType.DMA((11,)),
        ],
        compiler_params=pltpu.CompilerParams(
            collective_id=0, has_side_effects=True, vmem_limit_bytes=63 * 2**20),
        name="butterfly",
    )(
        tokens,
        jnp.transpose(up_weight[0], (1, 0, 2)),
        jnp.transpose(down_weight[0], (1, 0, 2)),
        up_left, up_right[0], down_left[0], down_right,
    )


def from_partner(array, axis, bit):
    return lax.ppermute(array, axis, [(i, i ^ 1 << bit) for i in range(lax.axis_size(axis))])


def general(tokens, up_weight, down_weight, up_left, up_right, down_left, down_right):
    levels = lax.axis_size("feat").bit_length() - 1
    gathered = lax.all_gather(tokens, "tok", axis=0, tiled=True)
    pieces = [gathered]
    for level in range(levels):
        pieces.append(from_partner(gathered, "feat", level))
    stacked = jnp.stack(pieces, axis=1)
    code_part = jnp.dot(tokens, up_left, preferred_element_type=jnp.float32)
    code = lax.psum(code_part, "feat").astype(jnp.bfloat16)
    code = lax.all_gather(code, "tok", axis=0, tiled=True)
    pre = jnp.einsum("rkd,tkd->rt", up_weight[0], stacked, preferred_element_type=jnp.float32)
    pre = pre + lax.dot_general(
        up_right[0], code, (((1,), (1,)), ((), ())), preferred_element_type=jnp.float32
    )
    hidden = jax.nn.gelu(pre, approximate=False).astype(jnp.bfloat16)
    local_down = down_weight[0]
    terms = jnp.einsum("rt,rkd->tkd", hidden, local_down, preferred_element_type=jnp.float32)
    total = terms[:, 0, :]
    for level in range(levels):
        total = total + from_partner(terms[:, level + 1, :], "feat", level)
    back_part = lax.dot_general(
        hidden, down_left[0], (((0,), (0,)), ((), ())), preferred_element_type=jnp.float32
    )
    total, back = (
        lax.psum_scatter(total, "tok", scatter_dimension=0, tiled=True),
        lax.psum_scatter(back_part, "tok", scatter_dimension=0, tiled=True),
    )
    back = lax.psum(back, "feat")
    mixed = total + jnp.dot(
        back.astype(jnp.bfloat16), down_right, preferred_element_type=jnp.float32
    )
    return mixed.astype(jnp.bfloat16)


def per_device(tokens, up_weight, *rest):
    rows, db = tokens.shape
    small = (lax.axis_size("tok"), lax.axis_size("feat")) == (2 * PLANES, 4)
    fits = rows % 16 == 0 and db % 1024 == 0 and up_weight.shape[1] % 256 == 0
    fits = fits and up_weight.shape[1] * db * 8 <= 40 * 2**20
    form = fused if small and fits else general
    return form(tokens, up_weight, *rest)


def solution(mesh):
    return jax.shard_map(
        per_device,
        mesh=mesh,
        in_specs=(
            P("tok", "feat"),
            P("feat", "tok", None, None),
            P("feat", "tok", None, None),
            P("feat", None),
            P("feat", "tok", None),
            P("feat", "tok", None),
            P(None, "feat"),
        ),
        out_specs=P("tok", "feat"),
        check_vma=False,
    )
```
